512 devices in a mesh: row: 32 (over y_hi, z), col: 16 (over y_lo, x, core).
Axes of the slice: x: 4, y: 8 (y_hi: 4, y_lo: 2; y = y_hi * 2 + y_lo), z: 8, core: 2. Of those that a mesh axis runs over, the one named last changes fastest.
Arguments:
- q_proj: bfloat16 [4096, 8192], P('row', 'col'), may hold values from -6 to 6
- k_proj: bfloat16 [4096, 8192], P('row', 'col'), may hold values from -6 to 6
- v_proj: bfloat16 [4096, 8192], P('row', 'col'), may hold values from -6 to 6
- filters: float32 [128, 512], P(None, 'col'), may hold values from -0.5 to 0.5
- w_out: bfloat16 [8192, 4096], P('col', 'row'), may hold values from -0.125 to 0.125
- cotangent: bfloat16 [4096, 4096], P('row', 'col'), may hold values from -1.5 to 1.5
Outputs:
- projected: bfloat16 [4096, 4096], P('row', 'col')
- grad_q: bfloat16 [4096, 8192], P('row', 'col')
- grad_k: bfloat16 [4096, 8192], P('row', 'col')
- grad_v: bfloat16 [4096, 8192], P('row', 'col')
- grad_filters: float32 [128, 512], P(None, 'col')
- grad_w: float32 [8192, 4096], P('col', 'row')
The draws below stay inside these ranges and needn't reach their ends.
All inputs are finite; a program needn't handle non-finite values.
Results may differ from the reference program's by a relative error of at most 0.0058.
Values may be sent and summed in bfloat16 or wider, within the bound.
No kernel may reach another device: no remote copies, remote signals or barrier semaphores. Data moves between devices by JAX's collectives and lax.ppermute only.
A program may use at most 64 MiB of HBM per device.

```python
import jax
import jax.numpy as jnp
from jax import lax

D = 8192
TAPS = 128
GROUP = 16
TOKENS = 4096
GROUPS = 512
E = 4096


def spiked(entries, stream_key, source, target, blocks, factor):
    owner, partner = [(jnp.arange(entries.shape[axis_at]) // (entries.shape[axis_at] // blocks)).reshape([-1 if axis == axis_at else 1 for axis in range(entries.ndim)]) for axis_at in (source, target)]
    chosen = jax.random.permutation(stream_key, blocks)[partner]
    strong = (owner == chosen) | (owner == (partner + blocks // 2) % blocks)
    return jnp.where(strong, factor * entries, entries)


def block_scale(key, shape, split, low, top_value):
    loudness, own = 1.0, jax.random.fold_in(key, 6)
    for axis_at, blocks in split:
        draws = jnp.exp(jax.random.uniform(jax.random.fold_in(own, axis_at), (blocks,), jnp.float32, low / len(split), top_value / len(split)))
        loudness = loudness * jnp.repeat(draws, shape[axis_at] // blocks).reshape([-1 if axis == axis_at else 1 for axis in range(len(shape))])
    return loudness


def centred(stream_key, extent, scale, most, split=(), dtype=jnp.bfloat16):
    drawn = scale * jax.random.normal(stream_key, extent, jnp.float32)
    if split:
        drawn = drawn * block_scale(stream_key, extent, split, -0.22, 0.18)
    return jnp.clip(drawn, -most, most).astype(dtype)


def heavy_noise(rng, dims, width, bound, pieces, heavy, kind=jnp.bfloat16):
    entries = width * jax.random.normal(rng, dims, jnp.float32)
    if pieces:
        entries = entries * block_scale(rng, dims, pieces, -0.22, 0.18)
    return jnp.clip(spiked(entries, jax.random.fold_in(rng, 3), *heavy), -bound, bound).astype(kind)


def setup_inputs(seed: int = 0) -> dict:
    key_of = jax.random.split(jax.random.key(seed), 7)
    return {
        "q_proj": centred(key_of[0], (TOKENS, D), 1.0, 6.0, ((0, 32), (1, 16))),
        "k_proj": centred(key_of[1], (TOKENS, D), 1.0, 6.0, ((0, 32), (1, 16))),
        "v_proj": centred(key_of[2], (TOKENS, D), 1.0, 6.0, ((0, 32), (1, 16))),
        "filters": centred(key_of[3], (TAPS, GROUPS), TAPS ** -0.5, 0.5, ((1, 16),), jnp.float32),
        "w_out": heavy_noise(key_of[4], (D, E), D ** -0.5, 0.125, ((0, 16), (1, 32)), (0, 1, 32, 2.75)),
        "cotangent": heavy_noise(key_of[5], (TOKENS, E), 0.25, 1.5, ((0, 32), (1, 16)), (0, 1, 32, 2.75)),
    }


def reference(q_proj, k_proj, v_proj, filters, w_out, cotangent):
    taps_full = jnp.repeat(filters, GROUP, axis=1)
    product = (k_proj.astype(jnp.float32) * v_proj.astype(jnp.float32)).astype(jnp.bfloat16)
    padded = jnp.concatenate([jnp.zeros((TAPS - 1, D), jnp.float32), product.astype(jnp.float32)], 0)

    def forward_tap(index, acc):
        weights = lax.dynamic_index_in_dim(taps_full, index, 0, keepdims=False)
        begin = (TAPS - 1 - index).astype(jnp.int32)
        return acc + weights[None, :] * lax.dynamic_slice_in_dim(padded, begin, TOKENS, 0)

    conv = lax.fori_loop(jnp.int32(0), jnp.int32(TAPS), forward_tap, jnp.zeros((TOKENS, D), jnp.float32))
    mixed = (q_proj.astype(jnp.float32) * conv).astype(jnp.bfloat16)
    projected = jnp.dot(mixed, w_out, preferred_element_type=jnp.float32).astype(jnp.bfloat16)
    grad_mixed = jnp.dot(cotangent, w_out.T, preferred_element_type=jnp.float32)
    grad_q = (grad_mixed * conv).astype(jnp.bfloat16)
    grad_conv = grad_mixed * q_proj.astype(jnp.float32)
    grad_padded = jnp.concatenate([grad_conv, jnp.zeros((TAPS - 1, D), jnp.float32)], 0)

    def backward_tap(index, carry):
        grad_product, grad_taps = carry
        weights = lax.dynamic_index_in_dim(taps_full, index, 0, keepdims=False)
        grad_product = grad_product + weights[None, :] * lax.dynamic_slice_in_dim(grad_padded, index.astype(jnp.int32), TOKENS, 0)
        begin = (TAPS - 1 - index).astype(jnp.int32)
        line = jnp.sum(grad_conv * lax.dynamic_slice_in_dim(padded, begin, TOKENS, 0), axis=0)
        line = jnp.sum(line.reshape(GROUPS, GROUP), axis=1)
        grad_taps = lax.dynamic_update_slice(grad_taps, line[None, :], (index.astype(jnp.int32), jnp.int32(0)))
        return grad_product, grad_taps

    grad_product, grad_filters = lax.fori_loop(jnp.int32(0), jnp.int32(TAPS), backward_tap, (jnp.zeros((TOKENS, D), jnp.float32), jnp.zeros((TAPS, GROUPS), jnp.float32)))
    grad_k = (grad_product * v_proj.astype(jnp.float32)).astype(jnp.bfloat16)
    grad_v = (grad_product * k_proj.astype(jnp.float32)).astype(jnp.bfloat16)
    grad_w = jnp.dot(mixed.T, cotangent, preferred_element_type=jnp.float32)
    return projected, grad_q, grad_k, grad_v, grad_filters, grad_w
```

```python
import functools

import jax
import jax.numpy as jnp
from jax import lax
from jax.experimental import pallas as pl
from jax.experimental.pallas import tpu as pltpu
from jax.sharding import PartitionSpec as P

YS, ZS, COLS = 4, 8, 16
F32, BF16 = jnp.float32, jnp.bfloat16
NT = (((1,), (1,)), ((), ()))
TN = (((0,), (0,)), ((), ()))
NN = (((1,), (0,)), ((), ()))
Z_GROUPS = [[y * ZS + z for z in range(ZS)] for y in range(YS)]
Y_GROUPS = [[y * ZS + z for y in range(YS)] for z in range(ZS)]
CHIP_GROUPS = [[2 * i + core for i in range(8)] for core in range(2)]


def call(body, out_shape, args, scratch=(), flops=0, position=None, after=()):
    outs = out_shape if isinstance(out_shape, (list, tuple)) else [out_shape]
    size = sum(a.size * a.dtype.itemsize for a in args) + sum(
        o.size * jnp.dtype(o.dtype).itemsize for o in outs
    )
    specs = [pl.BlockSpec(memory_space=pltpu.VMEM)] * len(args)
    n_args = len(args)
    operands = list(args)
    if position is not None:
        specs = [pl.BlockSpec(memory_space=pltpu.SMEM)] + specs
        operands = [position] + operands
        n_args += 1
    specs += [pl.BlockSpec(memory_space=pl.ANY)] * len(after)
    operands += list(after)

    def run(*refs):
        body(*refs[:n_args], *refs[n_args + len(after) :])

    return pl.pallas_call(
        run,
        out_shape=out_shape,
        in_specs=specs,
        scratch_shapes=list(scratch),
        compiler_params=pltpu.CompilerParams(vmem_limit_bytes=40 * 1024 * 1024),
        cost_estimate=pl.CostEstimate(flops=flops, bytes_accessed=size, transcendentals=0),
    )(*operands)


def shaped(shape, dtype):
    return jax.ShapeDtypeStruct(shape, dtype)


def iotas(rows, cols):
    return (
        lax.broadcasted_iota(jnp.int32, (rows, cols), 0),
        lax.broadcasted_iota(jnp.int32, (rows, cols), 1),
    )


def circulant(row):
    size = row.shape[1]
    return pltpu.roll(jnp.broadcast_to(row, (size, size)), 0, axis=1, stride=1, stride_axis=0)


def apply_filters(first_rows, keep_own, own, other, stack, out, exact):
    size = own.shape[0]
    lanes = lax.broadcasted_iota(jnp.int32, (size, 128), 1) // 16
    for tile in range(own.shape[1] // 128):
        cols = slice(tile * 128, tile * 128 + 128)
        for g in range(8):
            c = circulant(first_rows[tile * 8 + g : tile * 8 + g + 1, :])
            rows = slice(g * size, (g + 1) * size)
            for part in range(2 if exact else 1):
                rounded = c.astype(BF16).astype(F32)
                at = 2 * size * part
                stack[rows, at : at + size] = jnp.where(keep_own, rounded, 0.0).astype(BF16)
                stack[rows, at + size : at + 2 * size] = jnp.where(keep_own, 0.0, rounded).astype(BF16)
                c = c - rounded
        both = jnp.concatenate([own[:, cols], other[:, cols]] * (2 if exact else 1), 0)
        r = lax.dot_general(stack[...], both, NN, preferred_element_type=F32)
        acc = r[:size]
        for g in range(1, 8):
            acc = jnp.where(lanes == g, r[g * size : (g + 1) * size], acc)
        out[:, cols] = acc


def conv_body(rows_ref, product_ref, halo_ref, q_ref, conv_ref, mixed_ref, stack):
    row, lane = iotas(128, 128)
    apply_filters(rows_ref, lane <= row, product_ref, halo_ref, stack, conv_ref, True)
    mixed_ref[...] = (q_ref[...].astype(F32) * conv_ref[...]).astype(BF16)


def spread_body(piece_ref, out_ref):
    for i in range(8):
        out_ref[i] = piece_ref[...]


def grad_mixed_body(at_ref, own_ref, pair_ref, w_ref, cot_ref, out_ref):
    core = at_ref[1]
    for i in range(8):
        cot_ref[2 * i + core] = own_ref[i]
        cot_ref[2 * i + 1 - core] = pair_ref[i]
    w = jnp.concatenate([w_ref[z] for z in range(ZS)], 1)
    for y in range(YS):
        lhs = jnp.concatenate([cot_ref[4 * y + k] for k in range(4)], 1)
        out_ref[y] = lax.dot_general(lhs, w, NT, preferred_element_type=F32).astype(BF16)


def projected_body(at_ref, m0_ref, m1_ref, m2_ref, m3_ref, w_ref, keep_ref, give_ref, total):
    y, core = at_ref[0], at_ref[1]
    mixed = jnp.concatenate([m[...] for m in (m0_ref, m1_ref, m2_ref, m3_ref)], 0)
    for k in range(4):
        w = jnp.concatenate([w_ref[2 * k], w_ref[2 * k + 1]], 1)
        r = lax.dot_general(mixed, w, NN, preferred_element_type=F32)
        for d in range(YS):
            total[4 * lax.rem(y + YS - d, YS) + k] = r[d * 128 : d * 128 + 128]
    for i in range(8):
        keep_ref[i] = total[2 * i + core]
        give_ref[i] = total[2 * i + 1 - core].astype(BF16)


def pair_body(keep_ref, got_ref, out_ref):
    for i in range(8):
        out_ref[i] = (keep_ref[i] + got_ref[i].astype(F32)).astype(BF16)


def taps_body(taps_ref, out_ref):
    taps = taps_ref[...].astype(BF16)
    for i in range(YS * ZS):
        out_ref[i] = taps


def grad_w_body(at_ref, m0_ref, m1_ref, m2_ref, m3_ref, cot_ref, out_ref):
    mixed = jnp.concatenate([m[...] for m in (m0_ref, m1_ref, m2_ref, m3_ref)], 0)
    for k in range(4):
        cot = jnp.concatenate([cot_ref[4 * lax.rem(at_ref[0] + YS - d, YS) + k] for d in range(YS)], 0)
        r = lax.dot_general(mixed, cot, TN, preferred_element_type=F32).astype(BF16)
        out_ref[2 * k] = r[:, :128]
        out_ref[2 * k + 1] = r[:, 128:]


def grad_conv_body(shares_ref, q_ref, conv_ref, grad_q_ref, grad_conv_ref):
    g = shares_ref[0].astype(F32)
    for y in range(1, YS):
        g = g + shares_ref[y].astype(F32)
    grad_q_ref[...] = (g * conv_ref[...]).astype(BF16)
    grad_conv_ref[...] = (g * q_ref[...].astype(F32)).astype(BF16)


def grad_filters_body(grad_conv_ref, product_ref, halo_ref, out_ref, own_stack, halo_stack):
    row, lane = iotas(128, 128)
    flip = jnp.where(row + lane == 127, 1.0, 0.0).astype(BF16)
    own_part = row + lane <= 127
    group = lane // 16
    for tile in range(4):
        cols = slice(tile * 128, tile * 128 + 128)
        reverse = lax.dot_general(
            flip, grad_conv_ref[:, cols], NN, preferred_element_type=F32
        ).astype(BF16)
        own = product_ref[:, cols].astype(F32)
        halo = halo_ref[:, cols].astype(F32)
        for g in range(8):
            own_stack[g * 128 : g * 128 + 128, :] = jnp.where(group == g, own, 0.0).astype(BF16)
            halo_stack[g * 128 : g * 128 + 128, :] = jnp.where(group == g, halo, 0.0).astype(BF16)
        m_own = lax.dot_general(own_stack[...], reverse, NT, preferred_element_type=F32)
        m_halo = lax.dot_general(halo_stack[...], reverse, NT, preferred_element_type=F32)
        for g in range(8):
            rows = slice(g * 128, g * 128 + 128)
            m = jnp.where(own_part, m_own[rows], m_halo[rows])
            m = pltpu.roll(m, 0, axis=1, stride=1, stride_axis=0)
            out_ref[tile * 8 + g : tile * 8 + g + 1, :] = jnp.sum(m, axis=0, keepdims=True)


def grad_kv_body(rows_ref, grad_conv_ref, next_ref, k_ref, v_ref, grad_k_ref, grad_v_ref, stack, total):
    row, lane = iotas(128, 128)
    apply_filters(rows_ref, lane >= row, grad_conv_ref, next_ref, stack, total, False)
    grad_k_ref[...] = (total[...] * v_ref[...].astype(F32)).astype(BF16)
    grad_v_ref[...] = (total[...] * k_ref[...].astype(F32)).astype(BF16)


def shift_row(block, distance):
    n = YS * ZS
    return lax.ppermute(
        block, "row", [(i, i + distance) for i in range(n) if 0 <= i + distance < n]
    )


def shift_y(block, distance):
    route = [
        (y * ZS + z, (y + distance) % YS * ZS + z) for y in range(YS) for z in range(ZS)
    ]
    return lax.ppermute(block, "row", route)


def other_core(block):
    return lax.ppermute(block, "col", [(i, i ^ 1) for i in range(COLS)])


def exchange(blocks, axis, groups):
    return lax.all_to_all(blocks, axis, 0, 0, axis_index_groups=groups, tiled=True)


def swap_pieces(piece):
    route = []
    for y in range(YS):
        for z in range(ZS):
            for other in range(YS):
                for k in range(4):
                    route.append(((y * ZS + z) * COLS + 4 * other + k, (other * ZS + z) * COLS + 4 * y + k))
    return lax.ppermute(piece, ("row", "col"), route)


def local(q_proj, k_proj, v_proj, filters, w_out, cotangent):
    at = jnp.stack([lax.axis_index("row") // ZS, lax.axis_index("col") % 2]).astype(jnp.int32)
    tile = shaped((128, 512), BF16)
    w8 = lax.all_gather(w_out, "row", axis_index_groups=Z_GROUPS)
    product = (k_proj.astype(F32) * v_proj.astype(F32)).astype(BF16)
    halo = shift_row(product, 1)
    piece = swap_pieces(cotangent)
    taps = filters.T
    forward_rows = jnp.roll(jnp.flip(taps, 1), 1, axis=1)
    conv, mixed = call(
        conv_body,
        [shaped((128, 512), F32), tile],
        (forward_rows, product, halo, q_proj),
        [pltpu.VMEM((1024, 512), BF16)],
        flops=2 * 4096 * 512 * 128 * 4,
    )
    own8 = call(spread_body, shaped((8, 128, 256), BF16), (piece,), after=(mixed,))
    own8 = exchange(own8, "col", CHIP_GROUPS)
    pair8 = other_core(own8)
    mixed4 = [mixed] + [shift_y(mixed, d) for d in (1, 2, 3)]

    cot16, shares = call(
        grad_mixed_body,
        [shaped((COLS, 128, 256), BF16), shaped((YS, 128, 512), BF16)],
        (own8, pair8, w8),
        flops=2 * 512 * 512 * 1024,
        position=at,
    )
    sums = exchange(shares, "row", Y_GROUPS)
    gw8 = call(
        grad_w_body,
        shaped((ZS, 512, 128), BF16),
        (*mixed4, cot16),
        flops=2 * 512 * 512 * 1024,
        position=at,
        after=(shares,),
    )
    keep, give = call(
        projected_body,
        [shaped((8, 128, 256), F32), shaped((8, 128, 256), BF16)],
        (*mixed4, w8),
        [pltpu.VMEM((COLS, 128, 256), F32)],
        flops=2 * 512 * 512 * 1024,
        position=at,
        after=(gw8,),
    )
    pieces = call(pair_body, shaped((8, 128, 256), BF16), (keep, other_core(give)), after=(sums,))
    grad_q, grad_conv = call(grad_conv_body, [tile, tile], (sums, q_proj, conv), after=(give,))
    later = shift_row(grad_conv, -1)
    grad_taps = call(
        grad_filters_body,
        shaped((32, 128), F32),
        (grad_conv, product, halo),
        [pltpu.VMEM((1024, 128), BF16), pltpu.VMEM((1024, 128), BF16)],
        flops=2 * 1024 * 128 * 128 * 8,
    )
    grad_k, grad_v = call(
        grad_kv_body,
        [tile, tile],
        (taps, grad_conv, later, k_proj, v_proj),
        [pltpu.VMEM((1024, 256), BF16), pltpu.VMEM((128, 512), F32)],
        flops=2 * 4096 * 256 * 128 * 4,
    )

    got = exchange(pieces, "col", CHIP_GROUPS)
    grad_taps = call(taps_body, shaped((YS * ZS, 32, 128), BF16), (grad_taps,), after=(got, grad_k))
    grad_taps = jnp.sum(lax.all_to_all(grad_taps, "row", 0, 0, tiled=True).astype(F32), 0)
    grad_filters = jnp.flip(grad_taps, 1).T

    projected = swap_pieces(jnp.sum(got.astype(F32), 0).astype(BF16))
    grad_w = lax.psum_scatter(gw8, "row", axis_index_groups=Z_GROUPS).astype(F32)
    return (projected, grad_q, grad_k, grad_v, grad_filters, grad_w)


def solution(mesh):
    placed = (
        P("row", "col"),
        P("row", "col"),
        P("row", "col"),
        P(None, "col"),
        P("col", "row"),
        P("row", "col"),
    )
    return jax.shard_map(
        local,
        mesh=mesh,
        in_specs=placed,
        out_specs=(
            P("row", "col"),
            P("row", "col"),
            P("row", "col"),
            P("row", "col"),
            P(None, "col"),
            P("col", "row"),
        ),
        check_vma=False,
    )
```

```python
import functools

import jax
import jax.numpy as jnp
from jax import lax
from jax.experimental import pallas as pl
from jax.experimental.pallas import tpu as pltpu
from jax.sharding import PartitionSpec as P

YS, ZS, COLS = 4, 8, 16
F32, BF16 = jnp.float32, jnp.bfloat16
NT = (((1,), (1,)), ((), ()))
TN = (((0,), (0,)), ((), ()))
NN = (((1,), (0,)), ((), ()))
Z_GROUPS = [[y * ZS + z for z in range(ZS)] for y in range(YS)]
CHIP_GROUPS = [[2 * i + core for i in range(8)] for core in range(2)]


def call(body, out_shape, args, scratch=(), flops=0, position=None, after=()):
    outs = out_shape if isinstance(out_shape, (list, tuple)) else [out_shape]
    size = sum(a.size * a.dtype.itemsize for a in args) + sum(
        o.size * jnp.dtype(o.dtype).itemsize for o in outs
    )
    specs = [pl.BlockSpec(memory_space=pltpu.VMEM)] * len(args)
    n_args = len(args)
    operands = list(args)
    if position is not None:
        specs = [pl.BlockSpec(memory_space=pltpu.SMEM)] + specs
        operands = [position] + operands
        n_args += 1
    specs += [pl.BlockSpec(memory_space=pl.ANY)] * len(after)
    operands += list(after)

    def run(*refs):
        body(*refs[:n_args], *refs[n_args + len(after) :])

    return pl.pallas_call(
        run,
        out_shape=out_shape,
        in_specs=specs,
        scratch_shapes=list(scratch),
        compiler_params=pltpu.CompilerParams(vmem_limit_bytes=40 * 1024 * 1024),
        cost_estimate=pl.CostEstimate(flops=flops, bytes_accessed=size, transcendentals=0),
    )(*operands)


def shaped(shape, dtype):
    return jax.ShapeDtypeStruct(shape, dtype)


def iotas(rows, cols):
    return (
        lax.broadcasted_iota(jnp.int32, (rows, cols), 0),
        lax.broadcasted_iota(jnp.int32, (rows, cols), 1),
    )


def circulant(row):
    size = row.shape[1]
    return pltpu.roll(jnp.broadcast_to(row, (size, size)), 0, axis=1, stride=1, stride_axis=0)


def apply_filters(first_rows, keep_own, own, other, stack, out, exact):
    size = own.shape[0]
    lanes = lax.broadcasted_iota(jnp.int32, (size, 128), 1) // 16
    for tile in range(own.shape[1] // 128):
        cols = slice(tile * 128, tile * 128 + 128)
        for g in range(8):
            c = circulant(first_rows[tile * 8 + g : tile * 8 + g + 1, :])
            rows = slice(g * size, (g + 1) * size)
            for part in range(2 if exact else 1):
                rounded = c.astype(BF16).astype(F32)
                at = 2 * size * part
                stack[rows, at : at + size] = jnp.where(keep_own, rounded, 0.0).astype(BF16)
                stack[rows, at + size : at + 2 * size] = jnp.where(keep_own, 0.0, rounded).astype(BF16)
                c = c - rounded
        both = jnp.concatenate([own[:, cols], other[:, cols]] * (2 if exact else 1), 0)
        r = lax.dot_general(stack[...], both, NN, preferred_element_type=F32)
        acc = r[:size]
        for g in range(1, 8):
            acc = jnp.where(lanes == g, r[g * size : (g + 1) * size], acc)
        out[:, cols] = acc


def conv_body(rows_ref, product_ref, halo_ref, q_ref, conv_ref, mixed_ref, stack):
    row, lane = iotas(128, 128)
    apply_filters(rows_ref, lane <= row, product_ref, halo_ref, stack, conv_ref, True)
    mixed_ref[...] = (q_ref[...].astype(F32) * conv_ref[...]).astype(BF16)


def spread_body(piece_ref, out_ref):
    for i in range(8):
        out_ref[i] = piece_ref[...]


def grad_mixed_body(at_ref, own_ref, pair_ref, w_ref, cot_ref, *out_refs):
    y, core = at_ref[0], at_ref[1]
    for i in range(8):
        cot_ref[2 * i + core] = own_ref[i]
        cot_ref[2 * i + 1 - core] = pair_ref[i]
    w = jnp.concatenate([w_ref[z] for z in range(ZS)], 1)
    for d in range(YS):
        at = lax.rem(y + d, YS) * 4
        lhs = jnp.concatenate([cot_ref[at + k] for k in range(4)], 1)
        out_refs[d][...] = lax.dot_general(lhs, w, NT, preferred_element_type=F32).astype(BF16)


def projected_body(at_ref, m0_ref, m1_ref, m2_ref, m3_ref, w_ref, keep_ref, give_ref, total):
    y, core = at_ref[0], at_ref[1]
    mixed = jnp.concatenate([m[...] for m in (m0_ref, m1_ref, m2_ref, m3_ref)], 0)
    for k in range(4):
        w = jnp.concatenate([w_ref[2 * k], w_ref[2 * k + 1]], 1)
        r = lax.dot_general(mixed, w, NN, preferred_element_type=F32)
        for d in range(YS):
            total[4 * lax.rem(y + YS - d, YS) + k] = r[d * 128 : d * 128 + 128]
    for i in range(8):
        keep_ref[i] = total[2 * i + core]
        give_ref[i] = total[2 * i + 1 - core].astype(BF16)


def pair_body(keep_ref, got_ref, out_ref):
    for i in range(8):
        out_ref[i] = (keep_ref[i] + got_ref[i].astype(F32)).astype(BF16)


def taps_body(taps_ref, out_ref):
    taps = taps_ref[...].astype(BF16)
    for i in range(YS * ZS):
        out_ref[i] = taps


def grad_w_body(at_ref, m0_ref, m1_ref, m2_ref, m3_ref, cot_ref, out_ref):
    mixed = jnp.concatenate([m[...] for m in (m0_ref, m1_ref, m2_ref, m3_ref)], 0)
    for k in range(4):
        cot = jnp.concatenate([cot_ref[4 * lax.rem(at_ref[0] + YS - d, YS) + k] for d in range(YS)], 0)
        r = lax.dot_general(mixed, cot, TN, preferred_element_type=F32).astype(BF16)
        out_ref[2 * k] = r[:, :128]
        out_ref[2 * k + 1] = r[:, 128:]


def grad_conv_body(a_ref, b_ref, c_ref, d_ref, q_ref, conv_ref, grad_q_ref, grad_conv_ref):
    g = a_ref[...].astype(F32) + b_ref[...].astype(F32) + c_ref[...].astype(F32) + d_ref[...].astype(F32)
    grad_q_ref[...] = (g * conv_ref[...]).astype(BF16)
    grad_conv_ref[...] = (g * q_ref[...].astype(F32)).astype(BF16)


def grad_filters_body(grad_conv_ref, product_ref, halo_ref, out_ref, own_stack, halo_stack):
    row, lane = iotas(128, 128)
    flip = jnp.where(row + lane == 127, 1.0, 0.0).astype(BF16)
    own_part = row + lane <= 127
    group = lane // 16
    for tile in range(4):
        cols = slice(tile * 128, tile * 128 + 128)
        reverse = lax.dot_general(
            flip, grad_conv_ref[:, cols], NN, preferred_element_type=F32
        ).astype(BF16)
        own = product_ref[:, cols].astype(F32)
        halo = halo_ref[:, cols].astype(F32)
        for g in range(8):
            own_stack[g * 128 : g * 128 + 128, :] = jnp.where(group == g, own, 0.0).astype(BF16)
            halo_stack[g * 128 : g * 128 + 128, :] = jnp.where(group == g, halo, 0.0).astype(BF16)
        m_own = lax.dot_general(own_stack[...], reverse, NT, preferred_element_type=F32)
        m_halo = lax.dot_general(halo_stack[...], reverse, NT, preferred_element_type=F32)
        for g in range(8):
            rows = slice(g * 128, g * 128 + 128)
            m = jnp.where(own_part, m_own[rows], m_halo[rows])
            m = pltpu.roll(m, 0, axis=1, stride=1, stride_axis=0)
            out_ref[tile * 8 + g : tile * 8 + g + 1, :] = jnp.sum(m, axis=0, keepdims=True)


def grad_kv_body(rows_ref, grad_conv_ref, next_ref, k_ref, v_ref, grad_k_ref, grad_v_ref, stack, total):
    row, lane = iotas(128, 128)
    apply_filters(rows_ref, lane >= row, grad_conv_ref, next_ref, stack, total, False)
    grad_k_ref[...] = (total[...] * v_ref[...].astype(F32)).astype(BF16)
    grad_v_ref[...] = (total[...] * k_ref[...].astype(F32)).astype(BF16)


def shift_row(block, distance):
    n = YS * ZS
    return lax.ppermute(
        block, "row", [(i, i + distance) for i in range(n) if 0 <= i + distance < n]
    )


def shift_y(block, distance):
    route = [
        (y * ZS + z, (y + distance) % YS * ZS + z) for y in range(YS) for z in range(ZS)
    ]
    return lax.ppermute(block, "row", route)


def other_core(block):
    return lax.ppermute(block, "col", [(i, i ^ 1) for i in range(COLS)])


def exchange(blocks, axis, groups):
    return lax.all_to_all(blocks, axis, 0, 0, axis_index_groups=groups, tiled=True)


def swap_pieces(piece):
    route = []
    for y in range(YS):
        for z in range(ZS):
            for other in range(YS):
                for k in range(4):
                    route.append(((y * ZS + z) * COLS + 4 * other + k, (other * ZS + z) * COLS + 4 * y + k))
    return lax.ppermute(piece, ("row", "col"), route)


def local(q_proj, k_proj, v_proj, filters, w_out, cotangent):
    at = jnp.stack([lax.axis_index("row") // ZS, lax.axis_index("col") % 2]).astype(jnp.int32)
    tile = shaped((128, 512), BF16)
    w8 = lax.all_gather(w_out, "row", axis_index_groups=Z_GROUPS)
    product = (k_proj.astype(F32) * v_proj.astype(F32)).astype(BF16)
    halo = shift_row(product, 1)
    piece = swap_pieces(cotangent)
    taps = filters.T
    forward_rows = jnp.roll(jnp.flip(taps, 1), 1, axis=1)
    conv, mixed = call(
        conv_body,
        [shaped((128, 512), F32), tile],
        (forward_rows, product, halo, q_proj),
        [pltpu.VMEM((1024, 512), BF16)],
        flops=2 * 4096 * 512 * 128 * 4,
    )
    mixed4 = [mixed] + [shift_y(mixed, d) for d in (1, 2, 3)]
    own8 = call(spread_body, shaped((8, 128, 256), BF16), (piece,), after=mixed4[1:2])
    own8 = exchange(own8, "col", CHIP_GROUPS)
    pair8 = other_core(own8)

    cot16, *shares = call(
        grad_mixed_body,
        [shaped((COLS, 128, 256), BF16)] + [tile] * YS,
        (own8, pair8, w8),
        flops=2 * 512 * 512 * 1024,
        position=at,
    )
    sums = [shares[0]] + [shift_y(shares[d], d) for d in (1, 2, 3)]
    gw8 = call(
        grad_w_body,
        shaped((ZS, 512, 128), BF16),
        (*mixed4, cot16),
        flops=2 * 512 * 512 * 1024,
        position=at,
        after=(shares[1],),
    )
    keep, give = call(
        projected_body,
        [shaped((8, 128, 256), F32), shaped((8, 128, 256), BF16)],
        (*mixed4, w8),
        [pltpu.VMEM((COLS, 128, 256), F32)],
        flops=2 * 512 * 512 * 1024,
        position=at,
        after=[gw8] + sums[1:],
    )
    pieces = call(pair_body, shaped((8, 128, 256), BF16), (keep, other_core(give)))
    grad_q, grad_conv = call(grad_conv_body, [tile, tile], (*sums, q_proj, conv), after=(give,))
    later = shift_row(grad_conv, -1)
    grad_taps = call(
        grad_filters_body,
        shaped((32, 128), F32),
        (grad_conv, product, halo),
        [pltpu.VMEM((1024, 128), BF16), pltpu.VMEM((1024, 128), BF16)],
        flops=2 * 1024 * 128 * 128 * 8,
    )
    grad_k, grad_v = call(
        grad_kv_body,
        [tile, tile],
        (taps, grad_conv, later, k_proj, v_proj),
        [pltpu.VMEM((1024, 256), BF16), pltpu.VMEM((128, 512), F32)],
        flops=2 * 4096 * 256 * 128 * 4,
    )

    got = exchange(pieces, "col", CHIP_GROUPS)
    grad_taps = call(taps_body, shaped((YS * ZS, 32, 128), BF16), (grad_taps,), after=(got, grad_k))
    grad_taps = jnp.sum(lax.all_to_all(grad_taps, "row", 0, 0, tiled=True).astype(F32), 0)
    grad_filters = jnp.flip(grad_taps, 1).T

    projected = swap_pieces(jnp.sum(got.astype(F32), 0).astype(BF16))
    grad_w = lax.psum_scatter(gw8, "row", axis_index_groups=Z_GROUPS).astype(F32)
    return (projected, grad_q, grad_k, grad_v, grad_filters, grad_w)


def solution(mesh):
    placed = (
        P("row", "col"),
        P("row", "col"),
        P("row", "col"),
        P(None, "col"),
        P("col", "row"),
        P("row", "col"),
    )
    return jax.shard_map(
        local,
        mesh=mesh,
        in_specs=placed,
        out_specs=(
            P("row", "col"),
            P("row", "col"),
            P("row", "col"),
            P("row", "col"),
            P(None, "col"),
            P("col", "row"),
        ),
        check_vma=False,
    )
```

```python
import functools

import jax
import jax.numpy as jnp
from jax import lax
from jax.experimental import pallas as pl
from jax.experimental.pallas import tpu as pltpu
from jax.sharding import PartitionSpec as P

YS, ZS, COLS = 4, 8, 16
F32, BF16 = jnp.float32, jnp.bfloat16
NT = (((1,), (1,)), ((), ()))
TN = (((0,), (0,)), ((), ()))
NN = (((1,), (0,)), ((), ()))
Z_GROUPS = [[y * ZS + z for z in range(ZS)] for y in range(YS)]
CHIP_GROUPS = [[2 * i + core for i in range(8)] for core in range(2)]


def call(body, out_shape, args, scratch=(), flops=0, position=None, after=()):
    outs = out_shape if isinstance(out_shape, (list, tuple)) else [out_shape]
    size = sum(a.size * a.dtype.itemsize for a in args) + sum(
        o.size * jnp.dtype(o.dtype).itemsize for o in outs
    )
    specs = [pl.BlockSpec(memory_space=pltpu.VMEM)] * len(args)
    n_args = len(args)
    operands = list(args)
    if position is not None:
        specs = [pl.BlockSpec(memory_space=pltpu.SMEM)] + specs
        operands = [position] + operands
        n_args += 1
    specs += [pl.BlockSpec(memory_space=pl.ANY)] * len(after)
    operands += list(after)

    def run(*refs):
        body(*refs[:n_args], *refs[n_args + len(after) :])

    return pl.pallas_call(
        run,
        out_shape=out_shape,
        in_specs=specs,
        scratch_shapes=list(scratch),
        compiler_params=pltpu.CompilerParams(vmem_limit_bytes=40 * 1024 * 1024),
        cost_estimate=pl.CostEstimate(flops=flops, bytes_accessed=size, transcendentals=0),
    )(*operands)


def shaped(shape, dtype):
    return jax.ShapeDtypeStruct(shape, dtype)


def iotas(rows, cols):
    return (
        lax.broadcasted_iota(jnp.int32, (rows, cols), 0),
        lax.broadcasted_iota(jnp.int32, (rows, cols), 1),
    )


def circulant(row):
    size = row.shape[1]
    return pltpu.roll(jnp.broadcast_to(row, (size, size)), 0, axis=1, stride=1, stride_axis=0)


def apply_filters(first_rows, keep_own, own, other, stack, out, exact):
    size = own.shape[0]
    lanes = lax.broadcasted_iota(jnp.int32, (size, 128), 1) // 16
    for tile in range(own.shape[1] // 128):
        cols = slice(tile * 128, tile * 128 + 128)
        for g in range(8):
            c = circulant(first_rows[tile * 8 + g : tile * 8 + g + 1, :])
            rows = slice(g * size, (g + 1) * size)
            for part in range(2 if exact else 1):
                rounded = c.astype(BF16).astype(F32)
                at = 2 * size * part
                stack[rows, at : at + size] = jnp.where(keep_own, rounded, 0.0).astype(BF16)
                stack[rows, at + size : at + 2 * size] = jnp.where(keep_own, 0.0, rounded).astype(BF16)
                c = c - rounded
        both = jnp.concatenate([own[:, cols], other[:, cols]] * (2 if exact else 1), 0)
        r = lax.dot_general(stack[...], both, NN, preferred_element_type=F32)
        acc = r[:size]
        for g in range(1, 8):
            acc = jnp.where(lanes == g, r[g * size : (g + 1) * size], acc)
        out[:, cols] = acc


def conv_body(rows_ref, product_ref, halo_ref, q_ref, conv_ref, mixed_ref, stack):
    row, lane = iotas(128, 128)
    apply_filters(rows_ref, lane <= row, product_ref, halo_ref, stack, conv_ref, True)
    mixed_ref[...] = (q_ref[...].astype(F32) * conv_ref[...]).astype(BF16)


def spread_body(piece_ref, out_ref):
    for i in range(8):
        out_ref[i] = piece_ref[...]


def grad_mixed_body(at_ref, own_ref, pair_ref, w_ref, cot_ref, *out_refs):
    y, core = at_ref[0], at_ref[1]
    for i in range(8):
        cot_ref[2 * i + core] = own_ref[i]
        cot_ref[2 * i + 1 - core] = pair_ref[i]
    w = jnp.concatenate([w_ref[z] for z in range(ZS)], 1)
    for d in range(YS):
        at = lax.rem(y + d, YS) * 4
        lhs = jnp.concatenate([cot_ref[at + k] for k in range(4)], 1)
        out_refs[d][...] = lax.dot_general(lhs, w, NT, preferred_element_type=F32).astype(BF16)


def projected_body(at_ref, m0_ref, m1_ref, m2_ref, m3_ref, w_ref, keep_ref, give_ref, total):
    y, core = at_ref[0], at_ref[1]
    mixed = jnp.concatenate([m[...] for m in (m0_ref, m1_ref, m2_ref, m3_ref)], 0)
    for k in range(4):
        w = jnp.concatenate([w_ref[2 * k], w_ref[2 * k + 1]], 1)
        r = lax.dot_general(mixed, w, NN, preferred_element_type=F32)
        for d in range(YS):
            total[4 * lax.rem(y + YS - d, YS) + k] = r[d * 128 : d * 128 + 128]
    for i in range(8):
        keep_ref[i] = total[2 * i + core]
        give_ref[i] = total[2 * i + 1 - core].astype(BF16)


def pair_body(keep_ref, got_ref, out_ref):
    for i in range(8):
        out_ref[i] = (keep_ref[i] + got_ref[i].astype(F32)).astype(BF16)


def taps_body(taps_ref, out_ref):
    taps = taps_ref[...].astype(BF16)
    for i in range(YS * ZS):
        out_ref[i] = taps


def grad_w_body(at_ref, m0_ref, m1_ref, m2_ref, m3_ref, cot_ref, out_ref):
    mixed = jnp.concatenate([m[...] for m in (m0_ref, m1_ref, m2_ref, m3_ref)], 0)
    for k in range(4):
        cot = jnp.concatenate([cot_ref[4 * lax.rem(at_ref[0] + YS - d, YS) + k] for d in range(YS)], 0)
        r = lax.dot_general(mixed, cot, TN, preferred_element_type=F32).astype(BF16)
        out_ref[2 * k] = r[:, :128]
        out_ref[2 * k + 1] = r[:, 128:]


def grad_conv_body(a_ref, b_ref, c_ref, d_ref, q_ref, conv_ref, grad_q_ref, grad_conv_ref):
    g = a_ref[...].astype(F32) + b_ref[...].astype(F32) + c_ref[...].astype(F32) + d_ref[...].astype(F32)
    grad_q_ref[...] = (g * conv_ref[...]).astype(BF16)
    grad_conv_ref[...] = (g * q_ref[...].astype(F32)).astype(BF16)


def grad_filters_body(grad_conv_ref, product_ref, halo_ref, out_ref, own_stack, halo_stack):
    row, lane = iotas(128, 128)
    flip = jnp.where(row + lane == 127, 1.0, 0.0).astype(BF16)
    own_part = row + lane <= 127
    group = lane // 16
    for tile in range(4):
        cols = slice(tile * 128, tile * 128 + 128)
        reverse = lax.dot_general(
            flip, grad_conv_ref[:, cols], NN, preferred_element_type=F32
        ).astype(BF16)
        own = product_ref[:, cols].astype(F32)
        halo = halo_ref[:, cols].astype(F32)
        for g in range(8):
            own_stack[g * 128 : g * 128 + 128, :] = jnp.where(group == g, own, 0.0).astype(BF16)
            halo_stack[g * 128 : g * 128 + 128, :] = jnp.where(group == g, halo, 0.0).astype(BF16)
        m_own = lax.dot_general(own_stack[...], reverse, NT, preferred_element_type=F32)
        m_halo = lax.dot_general(halo_stack[...], reverse, NT, preferred_element_type=F32)
        for g in range(8):
            rows = slice(g * 128, g * 128 + 128)
            m = jnp.where(own_part, m_own[rows], m_halo[rows])
            m = pltpu.roll(m, 0, axis=1, stride=1, stride_axis=0)
            out_ref[tile * 8 + g : tile * 8 + g + 1, :] = jnp.sum(m, axis=0, keepdims=True)


def grad_kv_body(rows_ref, grad_conv_ref, next_ref, k_ref, v_ref, grad_k_ref, grad_v_ref, stack, total):
    row, lane = iotas(128, 128)
    apply_filters(rows_ref, lane >= row, grad_conv_ref, next_ref, stack, total, False)
    grad_k_ref[...] = (total[...] * v_ref[...].astype(F32)).astype(BF16)
    grad_v_ref[...] = (total[...] * k_ref[...].astype(F32)).astype(BF16)


def shift_row(block, distance):
    n = YS * ZS
    return lax.ppermute(
        block, "row", [(i, i + distance) for i in range(n) if 0 <= i + distance < n]
    )


def shift_y(block, distance):
    route = [
        (y * ZS + z, (y + distance) % YS * ZS + z) for y in range(YS) for z in range(ZS)
    ]
    return lax.ppermute(block, "row", route)


def other_core(block):
    return lax.ppermute(block, "col", [(i, i ^ 1) for i in range(COLS)])


def exchange(blocks, axis, groups):
    return lax.all_to_all(blocks, axis, 0, 0, axis_index_groups=groups, tiled=True)


def swap_pieces(piece):
    route = []
    for y in range(YS):
        for z in range(ZS):
            for other in range(YS):
                for k in range(4):
                    route.append(((y * ZS + z) * COLS + 4 * other + k, (other * ZS + z) * COLS + 4 * y + k))
    return lax.ppermute(piece, ("row", "col"), route)


def local(q_proj, k_proj, v_proj, filters, w_out, cotangent):
    at = jnp.stack([lax.axis_index("row") // ZS, lax.axis_index("col") % 2]).astype(jnp.int32)
    tile = shaped((128, 512), BF16)
    w8 = lax.all_gather(w_out, "row", axis_index_groups=Z_GROUPS)
    product = (k_proj.astype(F32) * v_proj.astype(F32)).astype(BF16)
    halo = shift_row(product, 1)
    piece = swap_pieces(cotangent)
    taps = filters.T
    forward_rows = jnp.roll(jnp.flip(taps, 1), 1, axis=1)
    conv, mixed = call(
        conv_body,
        [shaped((128, 512), F32), tile],
        (forward_rows, product, halo, q_proj),
        [pltpu.VMEM((1024, 512), BF16)],
        flops=2 * 4096 * 512 * 128 * 4,
        after=(piece,),
    )
    mixed4 = [mixed] + [shift_y(mixed, d) for d in (1, 2, 3)]
    own8 = call(spread_body, shaped((8, 128, 256), BF16), (piece,), after=mixed4[1:])
    own8 = exchange(own8, "col", CHIP_GROUPS)
    pair8 = other_core(own8)

    keep, give = call(
        projected_body,
        [shaped((8, 128, 256), F32), shaped((8, 128, 256), BF16)],
        (*mixed4, w8),
        [pltpu.VMEM((COLS, 128, 256), F32)],
        flops=2 * 512 * 512 * 1024,
        position=at,
    )
    cot16, *shares = call(
        grad_mixed_body,
        [shaped((COLS, 128, 256), BF16)] + [tile] * YS,
        (own8, pair8, w8),
        flops=2 * 512 * 512 * 1024,
        position=at,
        after=(give,),
    )
    sums = [shares[0]] + [shift_y(shares[d], d) for d in (1, 2, 3)]
    gw8 = call(
        grad_w_body,
        shaped((ZS, 512, 128), BF16),
        (*mixed4, cot16),
        flops=2 * 512 * 512 * 1024,
        position=at,
        after=(shares[1],),
    )
    pieces = call(pair_body, shaped((8, 128, 256), BF16), (keep, other_core(give)), after=sums[1:])
    grad_q, grad_conv = call(grad_conv_body, [tile, tile], (*sums, q_proj, conv))
    later = shift_row(grad_conv, -1)
    grad_taps = call(
        grad_filters_body,
        shaped((32, 128), F32),
        (grad_conv, product, halo),
        [pltpu.VMEM((1024, 128), BF16), pltpu.VMEM((1024, 128), BF16)],
        flops=2 * 1024 * 128 * 128 * 8,
    )
    grad_k, grad_v = call(
        grad_kv_body,
        [tile, tile],
        (taps, grad_conv, later, k_proj, v_proj),
        [pltpu.VMEM((1024, 256), BF16), pltpu.VMEM((128, 512), F32)],
        flops=2 * 4096 * 256 * 128 * 4,
    )

    got = exchange(pieces, "col", CHIP_GROUPS)
    grad_taps = call(taps_body, shaped((YS * ZS, 32, 128), BF16), (grad_taps,), after=(got, grad_k))
    grad_taps = jnp.sum(lax.all_to_all(grad_taps, "row", 0, 0, tiled=True).astype(F32), 0)
    grad_filters = jnp.flip(grad_taps, 1).T

    projected = swap_pieces(jnp.sum(got.astype(F32), 0).astype(BF16))
    grad_w = lax.psum_scatter(gw8, "row", axis_index_groups=Z_GROUPS).astype(F32)
    return (projected, grad_q, grad_k, grad_v, grad_filters, grad_w)


def solution(mesh):
    placed = (
        P("row", "col"),
        P("row", "col"),
        P("row", "col"),
        P(None, "col"),
        P("col", "row"),
        P("row", "col"),
    )
    return jax.shard_map(
        local,
        mesh=mesh,
        in_specs=placed,
        out_specs=(
            P("row", "col"),
            P("row", "col"),
            P("row", "col"),
            P("row", "col"),
            P(None, "col"),
            P("col", "row"),
        ),
        check_vma=False,
    )
```

```python
import jax
import jax.numpy as jnp
from jax import lax
from jax.experimental import pallas as pl
from jax.experimental.pallas import tpu as pltpu
from jax.sharding import PartitionSpec as P

YS, ZS, COLS = 4, 8, 16
F32, BF16 = jnp.float32, jnp.bfloat16
NT = (((1,), (1,)), ((), ()))
TN = (((0,), (0,)), ((), ()))
NN = (((1,), (0,)), ((), ()))
Z_GROUPS = [[y * ZS + z for z in range(ZS)] for y in range(YS)]
Y_GROUPS = [[y * ZS + z for y in range(YS)] for z in range(ZS)]
CHIP_GROUPS = [[2 * i + core for i in range(8)] for core in range(2)]


def call(body, out_shape, args, scratch=(), flops=0, position=None, after=()):
    outs = out_shape if isinstance(out_shape, (list, tuple)) else [out_shape]
    size = sum(a.size * a.dtype.itemsize for a in args) + sum(
        o.size * jnp.dtype(o.dtype).itemsize for o in outs
    )
    specs = [pl.BlockSpec(memory_space=pltpu.VMEM)] * len(args)
    n_args = len(args)
    operands = list(args)
    if position is not None:
        specs = [pl.BlockSpec(memory_space=pltpu.SMEM)] + specs
        operands = [position] + operands
        n_args += 1
    specs += [pl.BlockSpec(memory_space=pl.ANY)] * len(after)
    operands += list(after)

    def run(*refs):
        body(*refs[:n_args], *refs[n_args + len(after) :])

    return pl.pallas_call(
        run,
        out_shape=out_shape,
        in_specs=specs,
        scratch_shapes=list(scratch),
        compiler_params=pltpu.CompilerParams(vmem_limit_bytes=40 * 1024 * 1024),
        cost_estimate=pl.CostEstimate(flops=flops, bytes_accessed=size, transcendentals=0),
    )(*operands)


def shaped(shape, dtype):
    return jax.ShapeDtypeStruct(shape, dtype)


def iotas(rows, cols):
    return (
        lax.broadcasted_iota(jnp.int32, (rows, cols), 0),
        lax.broadcasted_iota(jnp.int32, (rows, cols), 1),
    )


def circulant(row):
    size = row.shape[1]
    return pltpu.roll(jnp.broadcast_to(row, (size, size)), 0, axis=1, stride=1, stride_axis=0)


def apply_filters(first_rows, keep_own, own, other, stack, out, exact):
    size = own.shape[0]
    lanes = lax.broadcasted_iota(jnp.int32, (size, 128), 1) // 16
    for tile in range(own.shape[1] // 128):
        cols = slice(tile * 128, tile * 128 + 128)
        for g in range(8):
            c = circulant(first_rows[tile * 8 + g : tile * 8 + g + 1, :])
            rows = slice(g * size, (g + 1) * size)
            for part in range(2 if exact else 1):
                rounded = c.astype(BF16).astype(F32)
                at = 2 * size * part
                stack[rows, at : at + size] = jnp.where(keep_own, rounded, 0.0).astype(BF16)
                stack[rows, at + size : at + 2 * size] = jnp.where(keep_own, 0.0, rounded).astype(BF16)
                c = c - rounded
        both = jnp.concatenate([own[:, cols], other[:, cols]] * (2 if exact else 1), 0)
        r = lax.dot_general(stack[...], both, NN, preferred_element_type=F32)
        acc = r[:size]
        for g in range(1, 8):
            acc = jnp.where(lanes == g, r[g * size : (g + 1) * size], acc)
        out[:, cols] = acc


def conv_body(rows_ref, product_ref, halo_ref, q_ref, conv_ref, mixed_ref, stack):
    row, lane = iotas(128, 128)
    apply_filters(rows_ref, lane <= row, product_ref, halo_ref, stack, conv_ref, True)
    mixed_ref[...] = (q_ref[...].astype(F32) * conv_ref[...]).astype(BF16)


def spread_body(block_ref, out_ref):
    for i in range(out_ref.shape[0]):
        out_ref[i] = block_ref[...]


def grad_mixed_body(at_ref, own_ref, pair_ref, w_ref, cot_ref, out_ref):
    core = at_ref[0]
    for i in range(8):
        cot_ref[2 * i + core] = own_ref[i]
        cot_ref[2 * i + 1 - core] = pair_ref[i]
    w = jnp.concatenate([w_ref[z] for z in range(ZS)], 1)
    for y in range(YS):
        lhs = jnp.concatenate([cot_ref[4 * y + k] for k in range(4)], 1)
        out_ref[y] = lax.dot_general(lhs, w, NT, preferred_element_type=F32).astype(BF16)


def projected_body(at_ref, mixed_ref, w_ref, keep_ref, give_ref, total):
    core = at_ref[0]
    mixed = jnp.concatenate([mixed_ref[y] for y in range(YS)], 0)
    for k in range(4):
        w = jnp.concatenate([w_ref[2 * k], w_ref[2 * k + 1]], 1)
        r = lax.dot_general(mixed, w, NN, preferred_element_type=F32)
        for y in range(YS):
            total[4 * y + k] = r[y * 128 : y * 128 + 128]
    for i in range(8):
        keep_ref[i] = total[2 * i + core]
        give_ref[i] = total[2 * i + 1 - core].astype(BF16)


def pair_body(keep_ref, got_ref, out_ref):
    for i in range(8):
        out_ref[i] = (keep_ref[i] + got_ref[i].astype(F32)).astype(BF16)


def taps_body(taps_ref, out_ref):
    taps = taps_ref[...].astype(BF16)
    for i in range(YS * ZS):
        out_ref[i] = taps


def grad_w_body(mixed_ref, cot_ref, out_ref):
    mixed = jnp.concatenate([mixed_ref[y] for y in range(YS)], 0)
    for k in range(4):
        cot = jnp.concatenate([cot_ref[4 * y + k] for y in range(YS)], 0)
        r = lax.dot_general(mixed, cot, TN, preferred_element_type=F32).astype(BF16)
        out_ref[2 * k] = r[:, :128]
        out_ref[2 * k + 1] = r[:, 128:]


def grad_conv_body(shares_ref, q_ref, conv_ref, grad_q_ref, grad_conv_ref):
    g = shares_ref[0].astype(F32)
    for y in range(1, YS):
        g = g + shares_ref[y].astype(F32)
    grad_q_ref[...] = (g * conv_ref[...]).astype(BF16)
    grad_conv_ref[...] = (g * q_ref[...].astype(F32)).astype(BF16)


def grad_filters_body(grad_conv_ref, product_ref, halo_ref, out_ref, own_stack, halo_stack):
    row, lane = iotas(128, 128)
    flip = jnp.where(row + lane == 127, 1.0, 0.0).astype(BF16)
    own_part = row + lane <= 127
    group = lane // 16
    for tile in range(4):
        cols = slice(tile * 128, tile * 128 + 128)
        reverse = lax.dot_general(
            flip, grad_conv_ref[:, cols], NN, preferred_element_type=F32
        ).astype(BF16)
        own = product_ref[:, cols].astype(F32)
        halo = halo_ref[:, cols].astype(F32)
        for g in range(8):
            own_stack[g * 128 : g * 128 + 128, :] = jnp.where(group == g, own, 0.0).astype(BF16)
            halo_stack[g * 128 : g * 128 + 128, :] = jnp.where(group == g, halo, 0.0).astype(BF16)
        m_own = lax.dot_general(own_stack[...], reverse, NT, preferred_element_type=F32)
        m_halo = lax.dot_general(halo_stack[...], reverse, NT, preferred_element_type=F32)
        for g in range(8):
            rows = slice(g * 128, g * 128 + 128)
            m = jnp.where(own_part, m_own[rows], m_halo[rows])
            m = pltpu.roll(m, 0, axis=1, stride=1, stride_axis=0)
            out_ref[tile * 8 + g : tile * 8 + g + 1, :] = jnp.sum(m, axis=0, keepdims=True)


def grad_kv_body(rows_ref, grad_conv_ref, next_ref, k_ref, v_ref, grad_k_ref, grad_v_ref, stack, total):
    row, lane = iotas(128, 128)
    apply_filters(rows_ref, lane >= row, grad_conv_ref, next_ref, stack, total, False)
    grad_k_ref[...] = (total[...] * v_ref[...].astype(F32)).astype(BF16)
    grad_v_ref[...] = (total[...] * k_ref[...].astype(F32)).astype(BF16)


def shift_row(block, distance):
    n = YS * ZS
    return lax.ppermute(
        block, "row", [(i, i + distance) for i in range(n) if 0 <= i + distance < n]
    )


def other_core(block):
    return lax.ppermute(block, "col", [(i, i ^ 1) for i in range(COLS)])


def exchange(blocks, axis, groups):
    return lax.all_to_all(blocks, axis, 0, 0, axis_index_groups=groups, tiled=True)


def swap_pieces(piece):
    route = []
    for y in range(YS):
        for z in range(ZS):
            for other in range(YS):
                for k in range(4):
                    route.append(((y * ZS + z) * COLS + 4 * other + k, (other * ZS + z) * COLS + 4 * y + k))
    return lax.ppermute(piece, ("row", "col"), route)


def local(q_proj, k_proj, v_proj, filters, w_out, cotangent):
    at = (lax.axis_index("col") % 2).astype(jnp.int32).reshape(1)
    tile = shaped((128, 512), BF16)
    w8 = lax.all_gather(w_out, "row", axis_index_groups=Z_GROUPS)
    product = (k_proj.astype(F32) * v_proj.astype(F32)).astype(BF16)
    halo = shift_row(product, 1)
    piece = swap_pieces(cotangent)
    taps = filters.T
    forward_rows = jnp.roll(jnp.flip(taps, 1), 1, axis=1)
    conv, mixed = call(
        conv_body,
        [shaped((128, 512), F32), tile],
        (forward_rows, product, halo, q_proj),
        [pltpu.VMEM((1024, 512), BF16)],
        flops=2 * 4096 * 512 * 128 * 4,
    )
    own8 = call(spread_body, shaped((8, 128, 256), BF16), (piece,), after=(mixed,))
    own8 = exchange(own8, "col", CHIP_GROUPS)
    pair8 = other_core(own8)
    mixed4 = call(spread_body, shaped((YS, 128, 512), BF16), (mixed,), after=(own8,))
    mixed4 = exchange(mixed4, "row", Y_GROUPS)

    cot16, shares = call(
        grad_mixed_body,
        [shaped((COLS, 128, 256), BF16), shaped((YS, 128, 512), BF16)],
        (own8, pair8, w8),
        flops=2 * 512 * 512 * 1024,
        position=at,
    )
    sums = exchange(shares, "row", Y_GROUPS)
    gw8 = call(
        grad_w_body,
        shaped((ZS, 512, 128), BF16),
        (mixed4, cot16),
        flops=2 * 512 * 512 * 1024,
        after=(shares,),
    )
    keep, give = call(
        projected_body,
        [shaped((8, 128, 256), F32), shaped((8, 128, 256), BF16)],
        (mixed4, w8),
        [pltpu.VMEM((COLS, 128, 256), F32)],
        flops=2 * 512 * 512 * 1024,
        position=at,
        after=(gw8,),
    )
    pieces = call(pair_body, shaped((8, 128, 256), BF16), (keep, other_core(give)), after=(sums,))
    grad_q, grad_conv = call(grad_conv_body, [tile, tile], (sums, q_proj, conv), after=(give,))
    later = shift_row(grad_conv, -1)
    grad_taps = call(
        grad_filters_body,
        shaped((32, 128), F32),
        (grad_conv, product, halo),
        [pltpu.VMEM((1024, 128), BF16), pltpu.VMEM((1024, 128), BF16)],
        flops=2 * 1024 * 128 * 128 * 8,
    )
    grad_k, grad_v = call(
        grad_kv_body,
        [tile, tile],
        (taps, grad_conv, later, k_proj, v_proj),
        [pltpu.VMEM((1024, 256), BF16), pltpu.VMEM((128, 512), F32)],
        flops=2 * 4096 * 256 * 128 * 4,
    )

    got = exchange(pieces, "col", CHIP_GROUPS)
    grad_taps = call(taps_body, shaped((YS * ZS, 32, 128), BF16), (grad_taps,), after=(got,))
    grad_taps = jnp.sum(lax.all_to_all(grad_taps, "row", 0, 0, tiled=True).astype(F32), 0)
    grad_filters = jnp.flip(grad_taps, 1).T

    projected = swap_pieces(jnp.sum(got.astype(F32), 0).astype(BF16))
    grad_w = lax.psum_scatter(gw8, "row", axis_index_groups=Z_GROUPS).astype(F32)
    return (projected, grad_q, grad_k, grad_v, grad_filters, grad_w)


def solution(mesh):
    placed = (
        P("row", "col"),
        P("row", "col"),
        P("row", "col"),
        P(None, "col"),
        P("col", "row"),
        P("row", "col"),
    )
    return jax.shard_map(
        local,
        mesh=mesh,
        in_specs=placed,
        out_specs=(
            P("row", "col"),
            P("row", "col"),
            P("row", "col"),
            P("row", "col"),
            P(None, "col"),
            P("col", "row"),
        ),
        check_vma=False,
    )
```

```python
import jax
import jax.numpy as jnp
from jax import lax
from jax.experimental import pallas as pl
from jax.experimental.pallas import tpu as pltpu
from jax.sharding import PartitionSpec as P

YS, ZS, COLS = 4, 8, 16
F32, BF16 = jnp.float32, jnp.bfloat16
NT = (((1,), (1,)), ((), ()))
TN = (((0,), (0,)), ((), ()))
NN = (((1,), (0,)), ((), ()))
Z_GROUPS = [[y * ZS + z for z in range(ZS)] for y in range(YS)]
Y_GROUPS = [[y * ZS + z for y in range(YS)] for z in range(ZS)]
CHIP_GROUPS = [[2 * i + core for i in range(8)] for core in range(2)]


def call(body, out_shape, args, scratch=(), flops=0, position=None, after=()):
    outs = out_shape if isinstance(out_shape, (list, tuple)) else [out_shape]
    size = sum(a.size * a.dtype.itemsize for a in args) + sum(
        o.size * jnp.dtype(o.dtype).itemsize for o in outs
    )
    specs = [pl.BlockSpec(memory_space=pltpu.VMEM)] * len(args)
    n_args = len(args)
    operands = list(args)
    if position is not None:
        specs = [pl.BlockSpec(memory_space=pltpu.SMEM)] + specs
        operands = [position] + operands
        n_args += 1
    specs += [pl.BlockSpec(memory_space=pl.ANY)] * len(after)
    operands += list(after)

    def run(*refs):
        body(*refs[:n_args], *refs[n_args + len(after) :])

    return pl.pallas_call(
        run,
        out_shape=out_shape,
        in_specs=specs,
        scratch_shapes=list(scratch),
        compiler_params=pltpu.CompilerParams(vmem_limit_bytes=40 * 1024 * 1024),
        cost_estimate=pl.CostEstimate(flops=flops, bytes_accessed=size, transcendentals=0),
    )(*operands)


def shaped(shape, dtype):
    return jax.ShapeDtypeStruct(shape, dtype)


def iotas(rows, cols):
    return (
        lax.broadcasted_iota(jnp.int32, (rows, cols), 0),
        lax.broadcasted_iota(jnp.int32, (rows, cols), 1),
    )


def circulant(row):
    size = row.shape[1]
    return pltpu.roll(jnp.broadcast_to(row, (size, size)), 0, axis=1, stride=1, stride_axis=0)


def apply_filters(first_rows, keep_own, own, other, stack, out, exact):
    size = own.shape[0]
    lanes = lax.broadcasted_iota(jnp.int32, (size, 128), 1) // 16
    for tile in range(own.shape[1] // 128):
        cols = slice(tile * 128, tile * 128 + 128)
        for g in range(8):
            c = circulant(first_rows[tile * 8 + g : tile * 8 + g + 1, :])
            rows = slice(g * size, (g + 1) * size)
            for part in range(2 if exact else 1):
                rounded = c.astype(BF16).astype(F32)
                at = 2 * size * part
                stack[rows, at : at + size] = jnp.where(keep_own, rounded, 0.0).astype(BF16)
                stack[rows, at + size : at + 2 * size] = jnp.where(keep_own, 0.0, rounded).astype(BF16)
                c = c - rounded
        both = jnp.concatenate([own[:, cols], other[:, cols]] * (2 if exact else 1), 0)
        r = lax.dot_general(stack[...], both, NN, preferred_element_type=F32)
        acc = r[:size]
        for g in range(1, 8):
            acc = jnp.where(lanes == g, r[g * size : (g + 1) * size], acc)
        out[:, cols] = acc


def conv_body(rows_ref, product_ref, halo_ref, q_ref, conv_ref, mixed_ref, stack):
    row, lane = iotas(128, 128)
    apply_filters(rows_ref, lane <= row, product_ref, halo_ref, stack, conv_ref, True)
    mixed = (q_ref[...].astype(F32) * conv_ref[...]).astype(BF16)
    for y in range(YS):
        mixed_ref[y] = mixed


def spread_body(block_ref, out_ref):
    for i in range(out_ref.shape[0]):
        out_ref[i] = block_ref[...]


def grad_mixed_body(at_ref, own_ref, pair_ref, w_ref, cot_ref, out_ref):
    core = at_ref[0]
    for i in range(8):
        cot_ref[2 * i + core] = own_ref[i]
        cot_ref[2 * i + 1 - core] = pair_ref[i]
    w = jnp.concatenate([w_ref[z] for z in range(ZS)], 1)
    for y in range(YS):
        lhs = jnp.concatenate([cot_ref[4 * y + k] for k in range(4)], 1)
        out_ref[y] = lax.dot_general(lhs, w, NT, preferred_element_type=F32).astype(BF16)


def projected_body(at_ref, mixed_ref, w_ref, keep_ref, give_ref, total):
    core = at_ref[0]
    mixed = jnp.concatenate([mixed_ref[y] for y in range(YS)], 0)
    for k in range(4):
        w = jnp.concatenate([w_ref[2 * k], w_ref[2 * k + 1]], 1)
        r = lax.dot_general(mixed, w, NN, preferred_element_type=F32)
        for y in range(YS):
            total[4 * y + k] = r[y * 128 : y * 128 + 128]
    for i in range(8):
        keep_ref[i] = total[2 * i + core]
        give_ref[i] = total[2 * i + 1 - core].astype(BF16)


def pair_body(keep_ref, got_ref, out_ref):
    for i in range(8):
        out_ref[i] = (keep_ref[i] + got_ref[i].astype(F32)).astype(BF16)


def taps_body(taps_ref, out_ref):
    taps = taps_ref[...].astype(BF16)
    for i in range(YS * ZS):
        out_ref[i] = taps


def grad_w_body(mixed_ref, cot_ref, out_ref):
    mixed = jnp.concatenate([mixed_ref[y] for y in range(YS)], 0)
    for k in range(4):
        cot = jnp.concatenate([cot_ref[4 * y + k] for y in range(YS)], 0)
        r = lax.dot_general(mixed, cot, TN, preferred_element_type=F32).astype(BF16)
        out_ref[2 * k] = r[:, :128]
        out_ref[2 * k + 1] = r[:, 128:]


def grad_conv_body(shares_ref, q_ref, conv_ref, grad_q_ref, grad_conv_ref):
    g = shares_ref[0].astype(F32)
    for y in range(1, YS):
        g = g + shares_ref[y].astype(F32)
    grad_q_ref[...] = (g * conv_ref[...]).astype(BF16)
    grad_conv_ref[...] = (g * q_ref[...].astype(F32)).astype(BF16)


def grad_filters_body(grad_conv_ref, product_ref, halo_ref, out_ref, own_stack, halo_stack):
    row, lane = iotas(128, 128)
    flip = jnp.where(row + lane == 127, 1.0, 0.0).astype(BF16)
    own_part = row + lane <= 127
    group = lane // 16
    for tile in range(4):
        cols = slice(tile * 128, tile * 128 + 128)
        reverse = lax.dot_general(
            flip, grad_conv_ref[:, cols], NN, preferred_element_type=F32
        ).astype(BF16)
        own = product_ref[:, cols].astype(F32)
        halo = halo_ref[:, cols].astype(F32)
        for g in range(8):
            own_stack[g * 128 : g * 128 + 128, :] = jnp.where(group == g, own, 0.0).astype(BF16)
            halo_stack[g * 128 : g * 128 + 128, :] = jnp.where(group == g, halo, 0.0).astype(BF16)
        m_own = lax.dot_general(own_stack[...], reverse, NT, preferred_element_type=F32)
        m_halo = lax.dot_general(halo_stack[...], reverse, NT, preferred_element_type=F32)
        for g in range(8):
            rows = slice(g * 128, g * 128 + 128)
            m = jnp.where(own_part, m_own[rows], m_halo[rows])
            m = pltpu.roll(m, 0, axis=1, stride=1, stride_axis=0)
            out_ref[tile * 8 + g : tile * 8 + g + 1, :] = jnp.sum(m, axis=0, keepdims=True)


def grad_kv_body(rows_ref, grad_conv_ref, next_ref, k_ref, v_ref, grad_k_ref, grad_v_ref, stack, total):
    row, lane = iotas(128, 128)
    apply_filters(rows_ref, lane >= row, grad_conv_ref, next_ref, stack, total, False)
    grad_k_ref[...] = (total[...] * v_ref[...].astype(F32)).astype(BF16)
    grad_v_ref[...] = (total[...] * k_ref[...].astype(F32)).astype(BF16)


def shift_row(block, distance):
    n = YS * ZS
    return lax.ppermute(
        block, "row", [(i, i + distance) for i in range(n) if 0 <= i + distance < n]
    )


def other_core(block):
    return lax.ppermute(block, "col", [(i, i ^ 1) for i in range(COLS)])


def exchange(blocks, axis, groups):
    return lax.all_to_all(blocks, axis, 0, 0, axis_index_groups=groups, tiled=True)


def swap_pieces(piece):
    route = []
    for y in range(YS):
        for z in range(ZS):
            for other in range(YS):
                for k in range(4):
                    route.append(((y * ZS + z) * COLS + 4 * other + k, (other * ZS + z) * COLS + 4 * y + k))
    return lax.ppermute(piece, ("row", "col"), route)


def local(q_proj, k_proj, v_proj, filters, w_out, cotangent):
    at = (lax.axis_index("col") % 2).astype(jnp.int32).reshape(1)
    tile = shaped((128, 512), BF16)
    w8 = lax.all_gather(w_out, "row", axis_index_groups=Z_GROUPS)
    product = (k_proj.astype(F32) * v_proj.astype(F32)).astype(BF16)
    halo = shift_row(product, 1)
    piece = swap_pieces(cotangent)
    taps = filters.T
    forward_rows = jnp.roll(jnp.flip(taps, 1), 1, axis=1)
    conv, mixed4 = call(
        conv_body,
        [shaped((128, 512), F32), shaped((YS, 128, 512), BF16)],
        (forward_rows, product, halo, q_proj),
        [pltpu.VMEM((1024, 512), BF16)],
        flops=2 * 4096 * 512 * 128 * 4,
    )
    mixed4 = exchange(mixed4, "row", Y_GROUPS)
    own8 = call(spread_body, shaped((8, 128, 256), BF16), (piece,), after=(mixed4,))
    own8 = exchange(own8, "col", CHIP_GROUPS)
    pair8 = other_core(own8)

    cot16, shares = call(
        grad_mixed_body,
        [shaped((COLS, 128, 256), BF16), shaped((YS, 128, 512), BF16)],
        (own8, pair8, w8),
        flops=2 * 512 * 512 * 1024,
        position=at,
    )
    sums = exchange(shares, "row", Y_GROUPS)
    gw8 = call(
        grad_w_body,
        shaped((ZS, 512, 128), BF16),
        (mixed4, cot16),
        flops=2 * 512 * 512 * 1024,
        after=(shares,),
    )
    keep, give = call(
        projected_body,
        [shaped((8, 128, 256), F32), shaped((8, 128, 256), BF16)],
        (mixed4, w8),
        [pltpu.VMEM((COLS, 128, 256), F32)],
        flops=2 * 512 * 512 * 1024,
        position=at,
        after=(gw8,),
    )
    pieces = call(pair_body, shaped((8, 128, 256), BF16), (keep, other_core(give)), after=(sums,))
    grad_q, grad_conv = call(grad_conv_body, [tile, tile], (sums, q_proj, conv), after=(give,))
    later = shift_row(grad_conv, -1)
    grad_taps = call(
        grad_filters_body,
        shaped((32, 128), F32),
        (grad_conv, product, halo),
        [pltpu.VMEM((1024, 128), BF16), pltpu.VMEM((1024, 128), BF16)],
        flops=2 * 1024 * 128 * 128 * 8,
    )
    grad_k, grad_v = call(
        grad_kv_body,
        [tile, tile],
        (taps, grad_conv, later, k_proj, v_proj),
        [pltpu.VMEM((1024, 256), BF16), pltpu.VMEM((128, 512), F32)],
        flops=2 * 4096 * 256 * 128 * 4,
    )

    got = exchange(pieces, "col", CHIP_GROUPS)
    grad_taps = call(taps_body, shaped((YS * ZS, 32, 128), BF16), (grad_taps,), after=(got, later))
    grad_taps = jnp.sum(lax.all_to_all(grad_taps, "row", 0, 0, tiled=True).astype(F32), 0)
    grad_filters = jnp.flip(grad_taps, 1).T

    projected = swap_pieces(jnp.sum(got.astype(F32), 0).astype(BF16))
    grad_w = lax.psum_scatter(gw8, "row", axis_index_groups=Z_GROUPS).astype(F32)
    return (projected, grad_q, grad_k, grad_v, grad_filters, grad_w)


def solution(mesh):
    placed = (
        P("row", "col"),
        P("row", "col"),
        P("row", "col"),
        P(None, "col"),
        P("col", "row"),
        P("row", "col"),
    )
    return jax.shard_map(
        local,
        mesh=mesh,
        in_specs=placed,
        out_specs=(
            P("row", "col"),
            P("row", "col"),
            P("row", "col"),
            P("row", "col"),
            P(None, "col"),
            P("col", "row"),
        ),
        check_vma=False,
    )
```

```python
import jax
import jax.numpy as jnp
from jax import lax
from jax.experimental import pallas as pl
from jax.experimental.pallas import tpu as pltpu
from jax.sharding import PartitionSpec as P

YS, ZS, COLS = 4, 8, 16
F32, BF16 = jnp.float32, jnp.bfloat16
NT = (((1,), (1,)), ((), ()))
TN = (((0,), (0,)), ((), ()))
NN = (((1,), (0,)), ((), ()))
Z_GROUPS = [[y * ZS + z for z in range(ZS)] for y in range(YS)]
Y_GROUPS = [[y * ZS + z for y in range(YS)] for z in range(ZS)]
CHIP_GROUPS = [[2 * i + core for i in range(8)] for core in range(2)]


def call(body, out_shape, args, scratch=(), flops=0, position=None, after=()):
    outs = out_shape if isinstance(out_shape, (list, tuple)) else [out_shape]
    size = sum(a.size * a.dtype.itemsize for a in args) + sum(
        o.size * jnp.dtype(o.dtype).itemsize for o in outs
    )
    specs = [pl.BlockSpec(memory_space=pltpu.VMEM)] * len(args)
    n_args = len(args)
    operands = list(args)
    if position is not None:
        specs = [pl.BlockSpec(memory_space=pltpu.SMEM)] + specs
        operands = [position] + operands
        n_args += 1
    specs += [pl.BlockSpec(memory_space=pl.ANY)] * len(after)
    operands += list(after)

    def run(*refs):
        body(*refs[:n_args], *refs[n_args + len(after) :])

    return pl.pallas_call(
        run,
        out_shape=out_shape,
        in_specs=specs,
        scratch_shapes=list(scratch),
        compiler_params=pltpu.CompilerParams(vmem_limit_bytes=40 * 1024 * 1024),
        cost_estimate=pl.CostEstimate(flops=flops, bytes_accessed=size, transcendentals=0),
    )(*operands)


def shaped(shape, dtype):
    return jax.ShapeDtypeStruct(shape, dtype)


def iotas(rows, cols):
    return (
        lax.broadcasted_iota(jnp.int32, (rows, cols), 0),
        lax.broadcasted_iota(jnp.int32, (rows, cols), 1),
    )


def circulant(row):
    size = row.shape[1]
    return pltpu.roll(jnp.broadcast_to(row, (size, size)), 0, axis=1, stride=1, stride_axis=0)


def apply_filters(first_rows, keep_own, own, other, stack, out, exact):
    size = own.shape[0]
    lanes = lax.broadcasted_iota(jnp.int32, (size, 128), 1) // 16
    for tile in range(own.shape[1] // 128):
        cols = slice(tile * 128, tile * 128 + 128)
        for g in range(8):
            c = circulant(first_rows[tile * 8 + g : tile * 8 + g + 1, :])
            rows = slice(g * size, (g + 1) * size)
            for part in range(2 if exact else 1):
                rounded = c.astype(BF16).astype(F32)
                at = 2 * size * part
                stack[rows, at : at + size] = jnp.where(keep_own, rounded, 0.0).astype(BF16)
                stack[rows, at + size : at + 2 * size] = jnp.where(keep_own, 0.0, rounded).astype(BF16)
                c = c - rounded
        both = jnp.concatenate([own[:, cols], other[:, cols]] * (2 if exact else 1), 0)
        r = lax.dot_general(stack[...], both, NN, preferred_element_type=F32)
        acc = r[:size]
        for g in range(1, 8):
            acc = jnp.where(lanes == g, r[g * size : (g + 1) * size], acc)
        out[:, cols] = acc


def conv_body(rows_ref, product_ref, halo_ref, q_ref, conv_ref, mixed_ref, stack):
    row, lane = iotas(128, 128)
    apply_filters(rows_ref, lane <= row, product_ref, halo_ref, stack, conv_ref, True)
    mixed_ref[...] = (q_ref[...].astype(F32) * conv_ref[...]).astype(BF16)


def spread_body(block_ref, out_ref):
    for i in range(out_ref.shape[0]):
        out_ref[i] = block_ref[...]


def grad_mixed_body(at_ref, own_ref, pair_ref, w_ref, cot_ref, out_ref):
    core = at_ref[0]
    for i in range(8):
        cot_ref[2 * i + core] = own_ref[i]
        cot_ref[2 * i + 1 - core] = pair_ref[i]
    w = jnp.concatenate([w_ref[z] for z in range(ZS)], 1)
    for y in range(YS):
        lhs = jnp.concatenate([cot_ref[4 * y + k] for k in range(4)], 1)
        out_ref[y] = lax.dot_general(lhs, w, NT, preferred_element_type=F32).astype(BF16)


def projected_body(at_ref, mixed_ref, w_ref, keep_ref, give_ref, total):
    core = at_ref[0]
    mixed = jnp.concatenate([mixed_ref[y] for y in range(YS)], 0)
    for k in range(4):
        w = jnp.concatenate([w_ref[2 * k], w_ref[2 * k + 1]], 1)
        r = lax.dot_general(mixed, w, NN, preferred_element_type=F32)
        for y in range(YS):
            total[4 * y + k] = r[y * 128 : y * 128 + 128]
    for i in range(8):
        keep_ref[i] = total[2 * i + core]
        give_ref[i] = total[2 * i + 1 - core].astype(BF16)


def pair_body(keep_ref, got_ref, out_ref):
    for i in range(8):
        out_ref[i] = (keep_ref[i] + got_ref[i].astype(F32)).astype(BF16)


def taps_body(taps_ref, out_ref):
    taps = taps_ref[...].astype(BF16)
    for i in range(YS * ZS):
        out_ref[i] = taps


def grad_w_body(mixed_ref, cot_ref, out_ref):
    mixed = jnp.concatenate([mixed_ref[y] for y in range(YS)], 0)
    for k in range(4):
        cot = jnp.concatenate([cot_ref[4 * y + k] for y in range(YS)], 0)
        r = lax.dot_general(mixed, cot, TN, preferred_element_type=F32).astype(BF16)
        out_ref[2 * k] = r[:, :128]
        out_ref[2 * k + 1] = r[:, 128:]


def grad_conv_body(shares_ref, q_ref, conv_ref, grad_q_ref, grad_conv_ref):
    g = shares_ref[0].astype(F32)
    for y in range(1, YS):
        g = g + shares_ref[y].astype(F32)
    grad_q_ref[...] = (g * conv_ref[...]).astype(BF16)
    grad_conv_ref[...] = (g * q_ref[...].astype(F32)).astype(BF16)


def grad_filters_body(grad_conv_ref, product_ref, halo_ref, out_ref, own_stack, halo_stack):
    row, lane = iotas(128, 128)
    flip = jnp.where(row + lane == 127, 1.0, 0.0).astype(BF16)
    own_part = row + lane <= 127
    group = lane // 16
    for tile in range(4):
        cols = slice(tile * 128, tile * 128 + 128)
        reverse = lax.dot_general(
            flip, grad_conv_ref[:, cols], NN, preferred_element_type=F32
        ).astype(BF16)
        own = product_ref[:, cols].astype(F32)
        halo = halo_ref[:, cols].astype(F32)
        for g in range(8):
            own_stack[g * 128 : g * 128 + 128, :] = jnp.where(group == g, own, 0.0).astype(BF16)
            halo_stack[g * 128 : g * 128 + 128, :] = jnp.where(group == g, halo, 0.0).astype(BF16)
        m_own = lax.dot_general(own_stack[...], reverse, NT, preferred_element_type=F32)
        m_halo = lax.dot_general(halo_stack[...], reverse, NT, preferred_element_type=F32)
        for g in range(8):
            rows = slice(g * 128, g * 128 + 128)
            m = jnp.where(own_part, m_own[rows], m_halo[rows])
            m = pltpu.roll(m, 0, axis=1, stride=1, stride_axis=0)
            out_ref[tile * 8 + g : tile * 8 + g + 1, :] = jnp.sum(m, axis=0, keepdims=True)


def grad_kv_body(rows_ref, grad_conv_ref, next_ref, k_ref, v_ref, grad_k_ref, grad_v_ref, stack, total):
    row, lane = iotas(128, 128)
    apply_filters(rows_ref, lane >= row, grad_conv_ref, next_ref, stack, total, False)
    grad_k_ref[...] = (total[...] * v_ref[...].astype(F32)).astype(BF16)
    grad_v_ref[...] = (total[...] * k_ref[...].astype(F32)).astype(BF16)


def shift_row(block, distance):
    n = YS * ZS
    return lax.ppermute(
        block, "row", [(i, i + distance) for i in range(n) if 0 <= i + distance < n]
    )


def other_core(block):
    return lax.ppermute(block, "col", [(i, i ^ 1) for i in range(COLS)])


def exchange(blocks, axis, groups):
    return lax.all_to_all(blocks, axis, 0, 0, axis_index_groups=groups, tiled=True)


def swap_pieces(piece):
    route = []
    for y in range(YS):
        for z in range(ZS):
            for other in range(YS):
                for k in range(4):
                    route.append(((y * ZS + z) * COLS + 4 * other + k, (other * ZS + z) * COLS + 4 * y + k))
    return lax.ppermute(piece, ("row", "col"), route)


def local(q_proj, k_proj, v_proj, filters, w_out, cotangent):
    at = (lax.axis_index("col") % 2).astype(jnp.int32).reshape(1)
    tile = shaped((128, 512), BF16)
    w8 = lax.all_gather(w_out, "row", axis_index_groups=Z_GROUPS)
    product = (k_proj.astype(F32) * v_proj.astype(F32)).astype(BF16)
    halo = shift_row(product, 1)
    piece = swap_pieces(cotangent)
    taps = filters.T
    forward_rows = jnp.roll(jnp.flip(taps, 1), 1, axis=1)
    conv, mixed = call(
        conv_body,
        [shaped((128, 512), F32), tile],
        (forward_rows, product, halo, q_proj),
        [pltpu.VMEM((1024, 512), BF16)],
        flops=2 * 4096 * 512 * 128 * 4,
    )
    own8 = call(spread_body, shaped((8, 128, 256), BF16), (piece,), after=(mixed,))
    own8 = exchange(own8, "col", CHIP_GROUPS)
    pair8 = other_core(own8)
    mixed4 = call(spread_body, shaped((YS, 128, 512), BF16), (mixed,), after=(own8,))
    mixed4 = exchange(mixed4, "row", Y_GROUPS)

    cot16, shares = call(
        grad_mixed_body,
        [shaped((COLS, 128, 256), BF16), shaped((YS, 128, 512), BF16)],
        (own8, pair8, w8),
        flops=2 * 512 * 512 * 1024,
        position=at,
    )
    sums = exchange(shares, "row", Y_GROUPS)
    gw8 = call(
        grad_w_body,
        shaped((ZS, 512, 128), BF16),
        (mixed4, cot16),
        flops=2 * 512 * 512 * 1024,
        after=(shares,),
    )
    keep, give = call(
        projected_body,
        [shaped((8, 128, 256), F32), shaped((8, 128, 256), BF16)],
        (mixed4, w8),
        [pltpu.VMEM((COLS, 128, 256), F32)],
        flops=2 * 512 * 512 * 1024,
        position=at,
        after=(gw8,),
    )
    pieces = call(pair_body, shaped((8, 128, 256), BF16), (keep, other_core(give)), after=(sums,))
    grad_q, grad_conv = call(grad_conv_body, [tile, tile], (sums, q_proj, conv), after=(give,))
    later = shift_row(grad_conv, -1)
    grad_taps = call(
        grad_filters_body,
        shaped((32, 128), F32),
        (grad_conv, product, halo),
        [pltpu.VMEM((1024, 128), BF16), pltpu.VMEM((1024, 128), BF16)],
        flops=2 * 1024 * 128 * 128 * 8,
    )
    grad_k, grad_v = call(
        grad_kv_body,
        [tile, tile],
        (taps, grad_conv, later, k_proj, v_proj),
        [pltpu.VMEM((1024, 256), BF16), pltpu.VMEM((128, 512), F32)],
        flops=2 * 4096 * 256 * 128 * 4,
    )

    got = exchange(pieces, "col", CHIP_GROUPS)
    grad_taps = call(taps_body, shaped((YS * ZS, 32, 128), BF16), (grad_taps,), after=(got, later))
    grad_taps = jnp.sum(lax.all_to_all(grad_taps, "row", 0, 0, tiled=True).astype(F32), 0)
    grad_filters = jnp.flip(grad_taps, 1).T

    projected = swap_pieces(jnp.sum(got.astype(F32), 0).astype(BF16))
    grad_w = lax.psum_scatter(gw8, "row", axis_index_groups=Z_GROUPS).astype(F32)
    return (projected, grad_q, grad_k, grad_v, grad_filters, grad_w)


def solution(mesh):
    placed = (
        P("row", "col"),
        P("row", "col"),
        P("row", "col"),
        P(None, "col"),
        P("col", "row"),
        P("row", "col"),
    )
    return jax.shard_map(
        local,
        mesh=mesh,
        in_specs=placed,
        out_specs=(
            P("row", "col"),
            P("row", "col"),
            P("row", "col"),
            P("row", "col"),
            P(None, "col"),
            P("col", "row"),
        ),
        check_vma=False,
    )
```

```python
import jax
import jax.numpy as jnp
from jax import lax
from jax.experimental import pallas as pl
from jax.experimental.pallas import tpu as pltpu
from jax.sharding import PartitionSpec as P

YS, ZS, COLS = 4, 8, 16
F32, BF16 = jnp.float32, jnp.bfloat16
NT = (((1,), (1,)), ((), ()))
TN = (((0,), (0,)), ((), ()))
NN = (((1,), (0,)), ((), ()))
Z_GROUPS = [[y * ZS + z for z in range(ZS)] for y in range(YS)]
Y_GROUPS = [[y * ZS + z for y in range(YS)] for z in range(ZS)]
CHIP_GROUPS = [[2 * i + core for i in range(8)] for core in range(2)]


def call(body, out_shape, args, scratch=(), flops=0, position=None, after=()):
    outs = out_shape if isinstance(out_shape, (list, tuple)) else [out_shape]
    size = sum(a.size * a.dtype.itemsize for a in args) + sum(
        o.size * jnp.dtype(o.dtype).itemsize for o in outs
    )
    specs = [pl.BlockSpec(memory_space=pltpu.VMEM)] * len(args)
    n_args = len(args)
    operands = list(args)
    if position is not None:
        specs = [pl.BlockSpec(memory_space=pltpu.SMEM)] + specs
        operands = [position] + operands
        n_args += 1
    specs += [pl.BlockSpec(memory_space=pl.ANY)] * len(after)
    operands += list(after)

    def run(*refs):
        body(*refs[:n_args], *refs[n_args + len(after) :])

    return pl.pallas_call(
        run,
        out_shape=out_shape,
        in_specs=specs,
        scratch_shapes=list(scratch),
        compiler_params=pltpu.CompilerParams(vmem_limit_bytes=40 * 1024 * 1024),
        cost_estimate=pl.CostEstimate(flops=flops, bytes_accessed=size, transcendentals=0),
    )(*operands)


def shaped(shape, dtype):
    return jax.ShapeDtypeStruct(shape, dtype)


def iotas(rows, cols):
    return (
        lax.broadcasted_iota(jnp.int32, (rows, cols), 0),
        lax.broadcasted_iota(jnp.int32, (rows, cols), 1),
    )


def circulant(row):
    size = row.shape[1]
    return pltpu.roll(jnp.broadcast_to(row, (size, size)), 0, axis=1, stride=1, stride_axis=0)


def apply_filters(first_rows, keep_own, own, other, stack, out, exact):
    size = own.shape[0]
    lanes = lax.broadcasted_iota(jnp.int32, (size, 128), 1) // 16
    for tile in range(own.shape[1] // 128):
        cols = slice(tile * 128, tile * 128 + 128)
        for g in range(8):
            c = circulant(first_rows[tile * 8 + g : tile * 8 + g + 1, :])
            rows = slice(g * size, (g + 1) * size)
            for part in range(2 if exact else 1):
                rounded = c.astype(BF16).astype(F32)
                at = 2 * size * part
                stack[rows, at : at + size] = jnp.where(keep_own, rounded, 0.0).astype(BF16)
                stack[rows, at + size : at + 2 * size] = jnp.where(keep_own, 0.0, rounded).astype(BF16)
                c = c - rounded
        both = jnp.concatenate([own[:, cols], other[:, cols]] * (2 if exact else 1), 0)
        r = lax.dot_general(stack[...], both, NN, preferred_element_type=F32)
        acc = r[:size]
        for g in range(1, 8):
            acc = jnp.where(lanes == g, r[g * size : (g + 1) * size], acc)
        out[:, cols] = acc


def conv_body(rows_ref, product_ref, halo_ref, q_ref, conv_ref, mixed_ref, stack):
    row, lane = iotas(128, 128)
    apply_filters(rows_ref, lane <= row, product_ref, halo_ref, stack, conv_ref, True)
    mixed_ref[...] = (q_ref[...].astype(F32) * conv_ref[...]).astype(BF16)


def spread_body(block_ref, out_ref):
    for i in range(out_ref.shape[0]):
        out_ref[i] = block_ref[...]


def grad_mixed_body(at_ref, own_ref, pair_ref, w_ref, cot_ref, out_ref):
    core = at_ref[0]
    for i in range(8):
        cot_ref[2 * i + core] = own_ref[i]
        cot_ref[2 * i + 1 - core] = pair_ref[i]
    w = jnp.concatenate([w_ref[z] for z in range(ZS)], 1)
    for y in range(YS):
        lhs = jnp.concatenate([cot_ref[4 * y + k] for k in range(4)], 1)
        out_ref[y] = lax.dot_general(lhs, w, NT, preferred_element_type=F32).astype(BF16)


def projected_body(at_ref, mixed_ref, w_ref, keep_ref, give_ref, total):
    core = at_ref[0]
    mixed = jnp.concatenate([mixed_ref[y] for y in range(YS)], 0)
    for k in range(4):
        w = jnp.concatenate([w_ref[2 * k], w_ref[2 * k + 1]], 1)
        r = lax.dot_general(mixed, w, NN, preferred_element_type=F32)
        for y in range(YS):
            total[4 * y + k] = r[y * 128 : y * 128 + 128]
    for i in range(8):
        keep_ref[i] = total[2 * i + core]
        give_ref[i] = total[2 * i + 1 - core].astype(BF16)


def pair_body(keep_ref, got_ref, out_ref):
    for i in range(8):
        out_ref[i] = (keep_ref[i] + got_ref[i].astype(F32)).astype(BF16)


def taps_body(taps_ref, out_ref):
    row, lane = iotas(128, 128)
    flip = jnp.where(row + lane == 127, 1.0, 0.0).astype(BF16)
    taps = lax.dot_general(
        taps_ref[...].astype(BF16), flip, NN, preferred_element_type=F32
    ).astype(BF16)
    for i in range(YS * ZS):
        out_ref[i] = taps


def grad_w_body(mixed_ref, cot_ref, out_ref):
    mixed = jnp.concatenate([mixed_ref[y] for y in range(YS)], 0)
    for k in range(4):
        cot = jnp.concatenate([cot_ref[4 * y + k] for y in range(YS)], 0)
        r = lax.dot_general(mixed, cot, TN, preferred_element_type=F32).astype(BF16)
        out_ref[2 * k] = r[:, :128]
        out_ref[2 * k + 1] = r[:, 128:]


def grad_conv_body(shares_ref, q_ref, conv_ref, grad_q_ref, grad_conv_ref):
    g = shares_ref[0].astype(F32)
    for y in range(1, YS):
        g = g + shares_ref[y].astype(F32)
    grad_q_ref[...] = (g * conv_ref[...]).astype(BF16)
    grad_conv_ref[...] = (g * q_ref[...].astype(F32)).astype(BF16)


def grad_filters_body(grad_conv_ref, product_ref, halo_ref, out_ref, own_stack, halo_stack):
    row, lane = iotas(128, 128)
    flip = jnp.where(row + lane == 127, 1.0, 0.0).astype(BF16)
    own_part = row + lane <= 127
    group = lane // 16
    for tile in range(4):
        cols = slice(tile * 128, tile * 128 + 128)
        reverse = lax.dot_general(
            flip, grad_conv_ref[:, cols], NN, preferred_element_type=F32
        ).astype(BF16)
        own = product_ref[:, cols].astype(F32)
        halo = halo_ref[:, cols].astype(F32)
        for g in range(8):
            own_stack[g * 128 : g * 128 + 128, :] = jnp.where(group == g, own, 0.0).astype(BF16)
            halo_stack[g * 128 : g * 128 + 128, :] = jnp.where(group == g, halo, 0.0).astype(BF16)
        m_own = lax.dot_general(own_stack[...], reverse, NT, preferred_element_type=F32)
        m_halo = lax.dot_general(halo_stack[...], reverse, NT, preferred_element_type=F32)
        for g in range(8):
            rows = slice(g * 128, g * 128 + 128)
            m = jnp.where(own_part, m_own[rows], m_halo[rows])
            m = pltpu.roll(m, 0, axis=1, stride=1, stride_axis=0)
            out_ref[tile * 8 + g : tile * 8 + g + 1, :] = jnp.sum(m, axis=0, keepdims=True)


def grad_kv_body(rows_ref, grad_conv_ref, next_ref, k_ref, v_ref, grad_k_ref, grad_v_ref, stack, total):
    row, lane = iotas(128, 128)
    apply_filters(rows_ref, lane >= row, grad_conv_ref, next_ref, stack, total, False)
    grad_k_ref[...] = (total[...] * v_ref[...].astype(F32)).astype(BF16)
    grad_v_ref[...] = (total[...] * k_ref[...].astype(F32)).astype(BF16)


def shift_row(block, distance):
    n = YS * ZS
    return lax.ppermute(
        block, "row", [(i, i + distance) for i in range(n) if 0 <= i + distance < n]
    )


def other_core(block):
    return lax.ppermute(block, "col", [(i, i ^ 1) for i in range(COLS)])


def exchange(blocks, axis, groups):
    return lax.all_to_all(blocks, axis, 0, 0, axis_index_groups=groups, tiled=True)


def swap_pieces(piece):
    route = []
    for y in range(YS):
        for z in range(ZS):
            for other in range(YS):
                for k in range(4):
                    route.append(((y * ZS + z) * COLS + 4 * other + k, (other * ZS + z) * COLS + 4 * y + k))
    return lax.ppermute(piece, ("row", "col"), route)


def local(q_proj, k_proj, v_proj, filters, w_out, cotangent):
    at = (lax.axis_index("col") % 2).astype(jnp.int32).reshape(1)
    tile = shaped((128, 512), BF16)
    w8 = lax.all_gather(w_out, "row", axis_index_groups=Z_GROUPS)
    product = (k_proj.astype(F32) * v_proj.astype(F32)).astype(BF16)
    halo = shift_row(product, 1)
    piece = swap_pieces(cotangent)
    taps = filters.T
    forward_rows = jnp.roll(jnp.flip(taps, 1), 1, axis=1)
    conv, mixed = call(
        conv_body,
        [shaped((128, 512), F32), tile],
        (forward_rows, product, halo, q_proj),
        [pltpu.VMEM((1024, 512), BF16)],
        flops=2 * 4096 * 512 * 128 * 4,
    )
    own8 = call(spread_body, shaped((8, 128, 256), BF16), (piece,), after=(mixed,))
    own8 = exchange(own8, "col", CHIP_GROUPS)
    pair8 = other_core(own8)
    mixed4 = call(spread_body, shaped((YS, 128, 512), BF16), (mixed,), after=(own8,))
    mixed4 = exchange(mixed4, "row", Y_GROUPS)

    cot16, shares = call(
        grad_mixed_body,
        [shaped((COLS, 128, 256), BF16), shaped((YS, 128, 512), BF16)],
        (own8, pair8, w8),
        flops=2 * 512 * 512 * 1024,
        position=at,
    )
    sums = exchange(shares, "row", Y_GROUPS)
    keep, give = call(
        projected_body,
        [shaped((8, 128, 256), F32), shaped((8, 128, 256), BF16)],
        (mixed4, w8),
        [pltpu.VMEM((COLS, 128, 256), F32)],
        flops=2 * 512 * 512 * 1024,
        position=at,
        after=(shares,),
    )
    gw8 = call(
        grad_w_body,
        shaped((ZS, 512, 128), BF16),
        (mixed4, cot16),
        flops=2 * 512 * 512 * 1024,
        after=(give,),
    )
    pieces = call(pair_body, shaped((8, 128, 256), BF16), (keep, other_core(give)), after=(sums,))
    grad_q, grad_conv = call(grad_conv_body, [tile, tile], (sums, q_proj, conv), after=(gw8,))
    later = shift_row(grad_conv, -1)
    grad_taps = call(
        grad_filters_body,
        shaped((32, 128), F32),
        (grad_conv, product, halo),
        [pltpu.VMEM((1024, 128), BF16), pltpu.VMEM((1024, 128), BF16)],
        flops=2 * 1024 * 128 * 128 * 8,
    )
    grad_k, grad_v = call(
        grad_kv_body,
        [tile, tile],
        (taps, grad_conv, later, k_proj, v_proj),
        [pltpu.VMEM((1024, 256), BF16), pltpu.VMEM((128, 512), F32)],
        flops=2 * 4096 * 256 * 128 * 4,
    )

    got = exchange(pieces, "col", CHIP_GROUPS)
    grad_taps = call(taps_body, shaped((YS * ZS, 32, 128), BF16), (grad_taps,), after=(got, later))
    grad_taps = jnp.sum(lax.all_to_all(grad_taps, "row", 0, 0, tiled=True).astype(F32), 0)
    grad_filters = grad_taps.T

    projected = swap_pieces(jnp.sum(got.astype(F32), 0).astype(BF16))
    grad_w = lax.psum_scatter(gw8, "row", axis_index_groups=Z_GROUPS).astype(F32)
    return (projected, grad_q, grad_k, grad_v, grad_filters, grad_w)


def solution(mesh):
    placed = (
        P("row", "col"),
        P("row", "col"),
        P("row", "col"),
        P(None, "col"),
        P("col", "row"),
        P("row", "col"),
    )
    return jax.shard_map(
        local,
        mesh=mesh,
        in_specs=placed,
        out_specs=(
            P("row", "col"),
            P("row", "col"),
            P("row", "col"),
            P("row", "col"),
            P(None, "col"),
            P("col", "row"),
        ),
        check_vma=False,
    )
```
